32 devices in a mesh: tm: 4 (over y, x), rows: 4 (over z), clips: 2 (over core).
Axes of the slice: x: 2, y: 2, z: 4, core: 2. Of those that a mesh axis runs over, the one named last changes fastest.
Arguments:
- features: bfloat16 [8, 32, 128, 128], P(('clips', 'tm'), 'rows'), parts along dimension 0, may hold values from -6 to 6
- conv_weight: bfloat16 [4, 3, 3, 128, 128], replicated, may hold values from -0.1875 to 0.1875
- conv_bias: float32 [4, 128], replicated, may hold values from -3 to 3
- seed_nodes: int32 [64], P('clips'), parts along dimension 0, may hold values from 0 to 4095, as said below
- targets: int32 [64], P('clips'), parts along dimension 0, may hold values from 0 to 4095, as said below
Outputs:
- embeddings: bfloat16 [8, 32, 128, 128], P(('clips', 'tm'), 'rows'), parts along dimension 0
- returned: float32 [4, 64, 32, 128], P('tm', 'clips', 'rows'), parts along dimension 1
- walk_loss: float32 [64], P('clips'), parts along dimension 0
The draws below stay inside these ranges and needn't reach their ends.
There are 2 independent parts, one for each index of `clips`. The reference program is written for one: setup_inputs(seed, part) draws one part's arguments, and reference() takes and returns one part's arrays. A program takes and returns all parts, laid end to end along the dimension named above; an argument that names none is the same for every part. Nothing has to cross between parts.
Inputs may be any that keep to these rules, and one draw needn't show every extreme that they name: `seed_nodes`: the node row * 128 + column where walker w starts in the first frame. `targets`: each target lies within 3 rows and 3 columns of its walker's seed node, inside the map, numbered likewise.
All inputs are finite; a program needn't handle non-finite values.
Results may differ from the reference program's by a relative error of at most 0.017.
Values may be sent and summed in bfloat16 or wider, within the bound.
No kernel may reach another device: no remote copies, remote signals or barrier semaphores. Data moves between devices by JAX's collectives and lax.ppermute only.
A program may use at most 64 MiB of HBM per device.

```python
import jax
import jax.numpy as jnp
from jax import lax

C = 128
W = 128
FD = 1
LAYERS = 4
RADIUS = 7
WALKERS = 32
FRAMES = 4
H = 32
N_TM = 4


def walker_spots(key):
    base_key = jax.random.fold_in(key, 31)
    seed_row = jax.random.randint(jax.random.fold_in(base_key, 1), (WALKERS,), 0, H)
    seed_col = jax.random.randint(jax.random.fold_in(base_key, 2), (WALKERS,), 0, W)
    shift_row = jax.random.randint(jax.random.fold_in(base_key, 3), (WALKERS,), -3, 4)
    shift_col = jax.random.randint(jax.random.fold_in(base_key, 4), (WALKERS,), -3, 4)
    target_row = jnp.clip(seed_row + shift_row, 0, H - 1)
    target_col = jnp.clip(seed_col + shift_col, 0, W - 1)
    return ((seed_row * W + seed_col).astype(jnp.int32), (target_row * W + target_col).astype(jnp.int32))


def draw_seed_nodes(key, part):
    return walker_spots(key)[0]


def draw_targets(key, part):
    return walker_spots(key)[1]


def level_of(own_key, shape, shards, low, high):
    def one(position, parts):
        draws = jax.random.uniform(jax.random.fold_in(jax.random.fold_in(own_key, 6), position), (parts,), jnp.float32, low / len(shards), high / len(shards))
        return jnp.repeat(jnp.exp(draws), shape[position] // parts).reshape((-1,) + (1,) * (len(shape) - position - 1))

    level = one(*shards[0])
    for cut in shards[1:]:
        level = level * one(*cut)
    return level


def noise(key, shape, scale, limit, shards=(), dtype=jnp.bfloat16):
    gain = level_of(key, shape, shards, -0.22, 0.18) if shards else 1.0
    array = jax.random.normal(key, shape, jnp.float32) * scale * gain
    return jnp.minimum(jnp.maximum(array, -limit), limit).astype(dtype)


def setup_inputs(seed: int = 0, part: int = 0) -> dict:
    streams_of = jax.random.split(jax.random.key(seed), 6)
    own_keys = jax.random.split(jax.random.fold_in(streams_of[5], part), 6)
    return {
        "features": noise(own_keys[0], (FRAMES, H, W, C), 1.0, 6.0, ((0, 4), (1, 4))),
        "conv_weight": noise(streams_of[1], (LAYERS, 3, 3, C, C), (9 * C) ** -0.5, 0.1875),
        "conv_bias": noise(streams_of[2], (LAYERS, C), 0.5, 3.0, (), jnp.float32),
        "seed_nodes": draw_seed_nodes(jax.random.fold_in(jax.random.fold_in(streams_of[5], part), 71), part),
        "targets": draw_targets(jax.random.fold_in(jax.random.fold_in(streams_of[5], part), 71), part),
    }


TAU = 0.07
NORM_EPS = 1e-06

def encode(features, conv_weight, conv_bias):
    hidden = features
    for layer_index in range(LAYERS):
        conv_out = lax.conv_general_dilated(hidden.astype(jnp.float32), conv_weight[layer_index].astype(jnp.float32), (1, 1), ((1, 1), (1, 1)), dimension_numbers=('NHWC', 'HWIO', 'NHWC'), precision=lax.Precision.HIGHEST)
        hidden = (hidden.astype(jnp.float32) + jax.nn.relu(conv_out + conv_bias[layer_index])).astype(jnp.bfloat16)
    scaled = hidden.astype(jnp.float32)
    return (scaled / jnp.sqrt(lax.optimization_barrier(jnp.sum(scaled * scaled, axis=-1, keepdims=True)) + NORM_EPS)).astype(jnp.bfloat16)

def window_weights(own_rows, other_padded, offset):
    total_rows = own_rows.shape[0]
    map_width = own_rows.shape[1]
    scores = jnp.einsum('ajc,akc->ajk', own_rows, other_padded[offset:offset + total_rows], precision=lax.Precision.HIGHEST)
    rows_other = jnp.arange(total_rows) + offset - RADIUS
    rows_ok = (rows_other >= 0) & (rows_other < total_rows)
    columns = jnp.arange(map_width)
    near_cols = jnp.abs(columns[:, None] - columns[None, :]) <= RADIUS
    in_window = rows_ok[:, None, None] & near_cols[None]
    return jnp.where(in_window, jnp.exp((scores - 1.0) / TAU), 0.0)

def advance(walker_prob, norm_own, norm_other, act_own, act_other):
    total_rows = walker_prob.shape[1]
    totals = jnp.zeros(walker_prob.shape[1:], jnp.float32)
    for offset in range(2 * RADIUS + 1):
        totals = totals + lax.optimization_barrier(jnp.sum(window_weights(norm_own, norm_other, offset), axis=2))
    share_prob = lax.optimization_barrier((walker_prob / totals[None]).astype(jnp.bfloat16)).astype(jnp.float32)
    padded = jnp.pad(share_prob, ((0, 0), (RADIUS, RADIUS), (0, 0)))
    moved_prob = jnp.zeros(walker_prob.shape, jnp.float32)
    for offset in range(2 * RADIUS + 1):
        weights = lax.optimization_barrier(window_weights(act_own, act_other, offset).astype(jnp.bfloat16)).astype(jnp.float32)
        moved_prob = moved_prob + jnp.einsum('bak,ajk->baj', padded[:, offset:offset + total_rows], weights, precision=lax.Precision.HIGHEST)
    return moved_prob

def reference(features, conv_weight, conv_bias, seed_nodes, targets):
    embeddings = encode(features, conv_weight, conv_bias)
    frames = embeddings.astype(jnp.float32)
    frame_count = frames.shape[0]
    total_rows = frames.shape[1]
    map_width = frames.shape[2]
    padded_frames = jnp.pad(frames, ((0, 0), (RADIUS, RADIUS), (0, 0), (0, 0)))
    node_ids = jnp.arange(total_rows * map_width).astype(jnp.int32)
    walker_prob = (seed_nodes[:, None] == node_ids[None]).astype(jnp.float32).reshape(-1, total_rows, map_width)
    for frame_index in range(frame_count - 1):
        walker_prob = advance(walker_prob, frames[frame_index], padded_frames[frame_index + 1], frames[frame_index + 1], padded_frames[frame_index])
    returned_list = [walker_prob] * N_TM
    for frame_index in reversed(range(frame_count - 1)):
        walker_prob = advance(walker_prob, frames[frame_index + 1], padded_frames[frame_index], frames[frame_index], padded_frames[frame_index + 1])
        if frame_index % FD == 0:
            returned_list[frame_index // FD] = walker_prob
    returned = jnp.stack(returned_list)
    flat_prob = returned[0].reshape(returned.shape[1], -1)
    picked = jnp.take_along_axis(flat_prob, targets[:, None].astype(jnp.int32), axis=1)[:, 0]
    walk_loss = -jnp.log(picked)
    return (embeddings, returned, walk_loss)
```

```python
import jax
import jax.numpy as jnp
from jax import lax
from jax.sharding import PartitionSpec as P

LAYERS = 4
RADIUS = 7
TAU = 0.07
NORM_EPS = 1e-06
AXES = ("tm", "rows")


def moved(x, hops, by):
    rows = lax.axis_size("rows")
    pairs = [
        (source * rows + r, target * rows + r + by)
        for source, target in hops
        for r in range(rows)
        if 0 <= r + by < rows
    ]
    return lax.ppermute(x, AXES, pairs)


def gathered(x, dim, hops, width):
    count = x.shape[dim]
    middle = x if hops[0][0] == hops[0][1] else moved(x, hops, 0)
    low = moved(lax.slice_in_dim(x, count - width, count, axis=dim), hops, 1)
    high = moved(lax.slice_in_dim(x, 0, width, axis=dim), hops, -1)
    return jnp.concatenate([low, middle, high], axis=dim)


def placed_at(part, before, count):
    return jnp.pad(part, ((0, 0), (before, count - before - part.shape[1]), (0, 0)))


def scattered(parts, hops):
    count = parts.shape[1] - 2 * RADIUS
    middle = moved(parts[:, RADIUS : RADIUS + count], hops, 0)
    up = moved(parts[:, :RADIUS], hops, -1)
    down = moved(parts[:, RADIUS + count :], hops, 1)
    return (
        middle.astype(jnp.float32)
        + placed_at(up.astype(jnp.float32), count - RADIUS, count)
        + placed_at(down.astype(jnp.float32), 0, count)
    )


def shared_margins(parts, hops, stride):
    span = parts.shape[1]
    total = parts.astype(jnp.float32)
    distance = 1
    while span - stride * distance > 0:
        overlap = span - stride * distance
        below = moved(parts[:, span - overlap :], hops, distance)
        above = moved(parts[:, :overlap], hops, -distance)
        total = total + placed_at(below.astype(jnp.float32), 0, span)
        total = total + placed_at(above.astype(jnp.float32), span - overlap, span)
        distance += 1
    return total


def encode_once(features, conv_weight, conv_bias):
    row_count = features.shape[1]
    total_rows = row_count * lax.axis_size("rows")
    frames = range(lax.axis_size("tm"))
    padded = gathered(features, 1, [(t, t) for t in frames], LAYERS)
    first_row = lax.axis_index("rows") * row_count - LAYERS
    for layer_index in range(LAYERS):
        conv_out = lax.conv_general_dilated(
            padded,
            conv_weight[layer_index],
            (1, 1),
            ((0, 0), (1, 1)),
            dimension_numbers=("NHWC", "HWIO", "NHWC"),
            preferred_element_type=jnp.float32,
        )
        updated = padded[:, 1:-1].astype(jnp.float32) + jax.nn.relu(
            conv_out + conv_bias[layer_index]
        )
        first_row = first_row + 1
        global_rows = first_row + jnp.arange(updated.shape[1])
        inside = (global_rows >= 0) & (global_rows < total_rows)
        padded = jnp.where(inside[None, :, None, None], updated, 0.0).astype(jnp.bfloat16)
    return padded


def normalize(hidden):
    scaled = hidden.astype(jnp.float32)
    return (scaled / jnp.sqrt(jnp.sum(scaled * scaled, axis=-1, keepdims=True) + NORM_EPS)).astype(
        jnp.bfloat16
    )


def pair_weights(own, margin, rows_ok):
    row_count, width, channels = own.shape
    span = margin.shape[0]
    scores = lax.dot_general(
        own.reshape(-1, channels),
        margin.reshape(-1, channels),
        (((1,), (1,)), ((), ())),
        preferred_element_type=jnp.float32,
    ).reshape(row_count, width, span, width)
    offset = jnp.arange(span)[None, :] - jnp.arange(row_count)[:, None]
    near_rows = (offset >= 0) & (offset <= 2 * RADIUS) & rows_ok[None, :]
    columns = jnp.arange(width)
    near_cols = jnp.abs(columns[:, None] - columns[None, :]) <= RADIUS
    in_window = near_rows[:, None, :, None] & near_cols[None, :, None, :]
    weights = jnp.where(in_window, jnp.exp((scores - 1.0) / TAU), 0.0)
    totals = jnp.sum(weights, axis=(2, 3))
    return weights.astype(jnp.bfloat16).reshape(row_count * width, span * width), totals


def spread(share, weights):
    count, _, width = share.shape
    out = jnp.dot(share.reshape(count, -1), weights, preferred_element_type=jnp.float32)
    return out.reshape(count, -1, width)


def collect(share, weights):
    count, _, width = share.shape
    out = lax.dot_general(
        share.reshape(count, -1),
        weights,
        (((1,), (1,)), ((), ())),
        preferred_element_type=jnp.float32,
    )
    return out.reshape(count, -1, width)


def local(features, conv_weight, conv_bias, seed_nodes, targets):
    bf16 = jnp.bfloat16
    hidden = encode_once(features, conv_weight, conv_bias)
    embeddings = normalize(hidden)
    own = embeddings[0]
    row_count, width, _ = own.shape
    groups = lax.axis_size("tm")
    bands = lax.axis_size("rows")
    time_index = lax.axis_index("tm")
    row_start = lax.axis_index("rows") * row_count
    walkers = seed_nodes.shape[0]
    last = groups - 2
    margin_rows = row_start - RADIUS + jnp.arange(row_count + 2 * RADIUS)
    rows_ok = (margin_rows >= 0) & (margin_rows < row_count * bands)

    after = gathered(own, 0, [(t + 1, t) for t in range(1, groups - 1)], RADIUS)
    before = gathered(own, 0, [(0, 1)], RADIUS)
    weights, out_total = pair_weights(own, after, rows_ok)
    first_weights, first_in_total = pair_weights(own, before, rows_ok)

    margin_ids = margin_rows[:, None] * width + jnp.arange(width)[None]
    margin_ids = jnp.where(rows_ok[:, None], margin_ids, -1)
    starts = jnp.concatenate([seed_nodes, targets])
    spots = (starts[:, None, None] == margin_ids[None]).astype(bf16)
    begun = collect(spots, first_weights)
    prob = begun[:walkers]
    scale_part = jnp.sum(prob, axis=(1, 2))
    adjoint = (begun[walkers:] / first_in_total[None]).astype(bf16)
    ones = jnp.ones((1, row_count, width), bf16)
    in_total = first_in_total
    adjoint_sum = begun[walkers:]
    for t in range(1, last):
        share = (prob / out_total[None]).astype(bf16)
        parts = spread(jnp.concatenate([share, adjoint, ones]), weights).astype(bf16)
        sums = scattered(parts, [(t, t + 1)])
        here = time_index == t + 1
        prob = jnp.where(here, sums[:walkers], prob)
        in_total = jnp.where(here, sums[2 * walkers], in_total)
        adjoint_sum = jnp.where(here, sums[walkers : 2 * walkers], adjoint_sum)
        adjoint = (adjoint_sum / in_total[None]).astype(bf16)
    share = (prob / out_total[None]).astype(bf16)
    parts = spread(jnp.concatenate([share, ones]), weights).astype(bf16)
    sums = shared_margins(parts, [(last, last)], row_count)
    final = sums[:walkers]
    ok = rows_ok[None, :, None]
    share = jnp.where(ok, final / jnp.where(ok, sums[walkers:], 1.0), 0.0).astype(bf16)
    back = collect(share, weights)
    returned = jnp.where(time_index == last, back, 0.0)
    share = (back / in_total[None]).astype(bf16)
    loss_part = jnp.sum(share.astype(jnp.float32) * adjoint_sum, axis=(1, 2))
    carried = jnp.where(time_index == last, loss_part, scale_part)
    for t in range(last, 1, -1):
        margin = gathered(share, 1, [(t, t - 1)], RADIUS)
        back = collect(margin, weights)
        returned = jnp.where(time_index == t - 1, back, returned)
        share = (back / in_total[None]).astype(bf16)
    tail = moved(final[:, RADIUS : RADIUS + row_count].astype(bf16), [(last, groups - 1)], 0)
    returned = jnp.where(time_index == groups - 1, tail.astype(jnp.float32), returned)

    summed = carried
    for by in range(1, bands):
        pairs = [(r, (r + by) % bands) for r in range(bands)]
        summed = summed + lax.ppermute(carried, "rows", pairs)
    loss_sum = jnp.where(time_index == last, summed, 0.0)
    scale_sum = jnp.where(time_index == 1, summed, 0.0)
    for by in range(1, groups):
        pairs = [(t, (t + by) % groups) for t in range(groups)]
        other = lax.ppermute(summed, "tm", pairs)
        source = (time_index - by) % groups
        loss_sum = loss_sum + jnp.where(source == last, other, 0.0)
        scale_sum = scale_sum + jnp.where(source == 1, other, 0.0)

    parts = spread(share, first_weights).astype(bf16)
    sums = scattered(parts, [(1, 0)])
    returned = jnp.where(time_index == 0, sums, returned)
    returned = returned / scale_sum[:, None, None]
    walk_loss = -jnp.log(loss_sum / scale_sum)
    return (embeddings, returned[None], walk_loss)


def solution(mesh):
    placed = (P(("clips", "tm"), "rows", None, None), P(), P(), P("clips"), P("clips"))
    return jax.shard_map(
        local,
        mesh=mesh,
        in_specs=placed,
        out_specs=(
            P(("clips", "tm"), "rows", None, None),
            P("tm", "clips", "rows", None),
            P("clips"),
        ),
        check_vma=False,
    )
```

```python
import functools
import math

import jax
import jax.numpy as jnp
from jax import lax
from jax.experimental import pallas as pl
from jax.experimental.pallas import tpu as pltpu
from jax.sharding import PartitionSpec as P

LAYERS = 4
RADIUS = 7
TAU = 0.07
NORM_EPS = 1e-06
AXES = ("tm", "rows")
SHARP = math.log2(math.e) / TAU
BF16 = jnp.bfloat16
F32 = jnp.float32
VMEM_BYTES = 40 * 2**20


def moved(x, hops, by):
    rows = lax.axis_size("rows")
    pairs = [
        (source * rows + r, target * rows + r + by)
        for source, target in hops
        for r in range(rows)
        if 0 <= r + by < rows
    ]
    return lax.ppermute(x, AXES, pairs)


def call(body, outs, args, scalars, scratch=(), flops=0):
    vmem = pl.BlockSpec(memory_space=pltpu.VMEM)
    return pl.pallas_call(
        body,
        out_shape=[jax.ShapeDtypeStruct(shape, dtype) for shape, dtype in outs],
        in_specs=[pl.BlockSpec(memory_space=pltpu.SMEM)] + [vmem] * len(args),
        out_specs=[vmem] * len(outs),
        scratch_shapes=list(scratch),
        compiler_params=pltpu.CompilerParams(vmem_limit_bytes=VMEM_BYTES),
        cost_estimate=pl.CostEstimate(flops=flops, bytes_accessed=1 << 20, transcendentals=0),
    )(scalars, *args)


def encode_kernel(
    info, low, own, high, weight, bias, emb, emb_top, emb_bottom, pairs, top, bottom, result
):
    count, width, channels = own.shape
    layers = weight.shape[0]
    margin = low.shape[0]
    first_row, total_rows = info[0], info[1]

    def source(i):
        if i < margin:
            return low[i]
        if i < margin + count:
            return own[i - margin]
        return high[i - margin - count]

    size = (count + 2 * margin) // 2
    for q in range(size):
        pairs[0, q] = jnp.concatenate([source(2 * q), source(2 * q + 1)], axis=1)
    column = lax.broadcasted_iota(jnp.int32, (width, 2 * channels), 0)
    lane = lax.broadcasted_iota(jnp.int32, (1, 2 * channels), 1)
    zero = jnp.zeros((channels, channels), BF16)
    for layer in range(layers):
        now, later = layer % 2, (layer + 1) % 2
        for kw in range(3):
            for s in range(2):
                for o in range(2):
                    at = (pl.ds(s * channels, channels), pl.ds((2 * kw + o) * channels, channels))
                    kh = s - o
                    top[at] = weight[layer, kh, kw] if 0 <= kh <= 2 else zero
                    kh = s - o + 2
                    bottom[at] = weight[layer, kh, kw] if 0 <= kh <= 2 else zero
        size -= 1
        flat = pairs[now, : size + 1].reshape((size + 1) * width, 2 * channels)
        result[: size * width] = jnp.dot(
            flat[: size * width], top[...], preferred_element_type=F32
        ) + jnp.dot(flat[width:], bottom[...], preferred_element_type=F32)
        both = jnp.concatenate([bias[layer : layer + 1], bias[layer : layer + 1]], axis=1)
        for q in range(size):
            rows = pl.ds(q * width, width)
            left = pltpu.roll(result[rows, : 2 * channels], 1, 0)
            right = pltpu.roll(result[rows, 4 * channels :], width - 1, 0)
            conv = result[rows, 2 * channels : 4 * channels] + both
            conv = conv + jnp.where(column > 0, left, 0.0)
            conv = conv + jnp.where(column < width - 1, right, 0.0)
            held = jnp.concatenate(
                [pairs[now, q, :, channels:], pairs[now, q + 1, :, :channels]], axis=1
            ).astype(F32)
            updated = held + jnp.maximum(conv, 0.0)
            row = first_row - margin + layer + 1 + 2 * q + jnp.where(lane >= channels, 1, 0)
            inside = (row >= 0) & (row < total_rows)
            pairs[later, q] = jnp.where(inside, updated, 0.0).astype(BF16)
    for q in range(count // 2):
        for o in range(2):
            hidden = pairs[layers % 2, q, :, o * channels : (o + 1) * channels].astype(F32)
            norm = jnp.sum(hidden * hidden, axis=1, keepdims=True) + NORM_EPS
            unit = (hidden * lax.rsqrt(norm)).astype(BF16)
            row = 2 * q + o
            emb[row] = unit
            if row < RADIUS:
                emb_top[row] = unit
            if row >= count - RADIUS:
                emb_bottom[row - (count - RADIUS)] = unit


def encode(info, low, own, high, weight, bias):
    count, width, channels = own.shape
    size = (count + 2 * LAYERS) // 2
    edge = ((RADIUS, width, channels), BF16)
    return call(
        encode_kernel,
        [((count, width, channels), BF16), edge, edge],
        [low, own, high, weight, bias],
        info,
        [
            pltpu.VMEM((2, size, width, 2 * channels), BF16),
            pltpu.VMEM((2 * channels, 6 * channels), BF16),
            pltpu.VMEM((2 * channels, 6 * channels), BF16),
            pltpu.VMEM(((size - 1) * width, 6 * channels), F32),
        ],
        flops=4 * 10**9,
    )


def band_shape(count, width):
    return (count // 2, 2 * width, (2 * RADIUS + 2) * width)


def fill_band(info, own, low, middle, high, margin, band):
    count, width, channels = own.shape
    span = count + 2 * RADIUS
    first_row, total_rows = info[0], info[1]
    margin[: RADIUS * width] = low[...].reshape(RADIUS * width, channels)
    margin[RADIUS * width : (RADIUS + count) * width] = middle[...].reshape(count * width, channels)
    margin[(RADIUS + count) * width :] = high[...].reshape(RADIUS * width, channels)
    here = lax.broadcasted_iota(jnp.int32, (width, width), 0)
    there = lax.broadcasted_iota(jnp.int32, (width, width), 1)
    near = jnp.where(jnp.abs(here - there) <= RADIUS, -SHARP, -1e30)
    none = jnp.zeros((width, width), BF16)
    flat = own[...].reshape(count * width, channels)
    for q in range(span // 2):
        shift = []
        for o in range(2):
            row = first_row - RADIUS + 2 * q + o
            ok = (row >= 0) & (row < total_rows)
            shift.append(near + jnp.where(ok, 0.0, -1e30))
        begin, end = max(0, q - RADIUS), min(count // 2, q + 1)
        scores = lax.dot_general(
            flat[2 * begin * width : 2 * end * width],
            margin[2 * q * width : 2 * (q + 1) * width],
            (((1,), (1,)), ((), ())),
            preferred_element_type=F32,
        )
        for p in range(begin, end):
            for a in range(2):
                for o in range(2):
                    offset = 2 * (q - p) + o - a
                    at = (p, pl.ds(a * width, width), pl.ds((2 * (q - p) + o) * width, width))
                    if 0 <= offset <= 2 * RADIUS:
                        first = (2 * (p - begin) + a) * width
                        score = scores[first : first + width, o * width : (o + 1) * width]
                        band[at] = jnp.exp2(score * SHARP + shift[o]).astype(BF16)
                    else:
                        band[at] = none


def collect(margin_of, band):
    parts = []
    for p in range(band.shape[0]):
        parts.append(
            lax.dot_general(
                margin_of(p), band[p], (((1,), (1,)), ((), ())), preferred_element_type=F32
            )
        )
    return jnp.concatenate(parts, axis=1)


def spread(share, band):
    pair_count, step, window = band.shape
    parts = []
    for q in range(pair_count + window // step - 1):
        total = None
        for p in range(max(0, q - window // step + 1), min(pair_count, q + 1)):
            term = jnp.dot(
                share[:, p * step : (p + 1) * step],
                band[p, :, (q - p) * step : (q - p + 1) * step],
                preferred_element_type=F32,
            )
            total = term if total is None else total + term
        parts.append(total)
    return jnp.concatenate(parts, axis=1)


def begin_kernel(info, own, low, middle, high, starts, band, begun, margin):
    fill_band(info, own, low, middle, high, margin, band)
    count, width, _ = own.shape
    window = band.shape[2]
    ids = (info[0] - RADIUS) * width + lax.broadcasted_iota(jnp.int32, (1, window), 1)

    def spots(p):
        hit = (starts[...] == ids + 2 * p * width) | (starts[...] < 0)
        return jnp.where(hit, 1.0, 0.0).astype(BF16)

    begun[...] = collect(spots, band)


def first_kernel(
    info, own, low, middle, high, begun, band, out_total, up, mid, down, scale, margin
):
    fill_band(info, own, low, middle, high, margin, band)
    count, width, _ = own.shape
    walkers = scale.shape[0]
    ones = jnp.ones((16, band.shape[2]), BF16)
    total = collect(lambda p: ones, band)[:8]
    out_total[...] = total
    start = begun[:walkers]
    scale[...] = jnp.broadcast_to(jnp.sum(start, axis=1, keepdims=True), scale.shape)
    share = (start / total[:1]).astype(BF16)
    adjoint = (begun[walkers : 2 * walkers] / begun[2 * walkers : 2 * walkers + 1]).astype(BF16)
    split(spread(jnp.concatenate([share, adjoint]), band), width, up, mid, down)


def split(parts, width, up, mid, down):
    edge, size = RADIUS * width, mid.shape[1]
    up[...] = parts[:, :edge].astype(BF16)
    mid[...] = parts[:, edge : edge + size].astype(BF16)
    down[...] = parts[:, edge + size :].astype(BF16)


def joined(up, mid, down, width, rows):
    size = mid.shape[1]
    edge = up.shape[1]
    none = jnp.zeros((rows, size - edge), F32)
    return (
        mid[:rows].astype(F32)
        + jnp.concatenate([none, up[:rows].astype(F32)], axis=1)
        + jnp.concatenate([down[:rows].astype(F32), none], axis=1)
    )


def turn_kernel(info, up, mid, down, band, out_total, whole, *pieces):
    walkers = mid.shape[0] // 2
    width = band.shape[1] // 2
    share = (joined(up, mid, down, width, walkers) / out_total[:1]).astype(BF16)
    row = lax.broadcasted_iota(jnp.int32, (8, share.shape[1]), 0)
    ones = jnp.where(row == 0, 1.0, 0.0).astype(BF16)
    parts = spread(jnp.concatenate([share, ones]), band).astype(BF16)
    whole[...] = parts
    for i in range(len(pieces) // 2):
        pieces[2 * i][...] = parts[:, parts.shape[1] - pieces[2 * i].shape[1] :]
        pieces[2 * i + 1][...] = parts[:, : pieces[2 * i + 1].shape[1]]


def back_kernel(info, adj_up, adj_mid, adj_down, band, begun, scale, whole, *rest):
    pieces, outs = rest[:-6], rest[-6:]
    back, top, share_out, bottom, carried, tail = outs
    walkers = scale.shape[0]
    width = band.shape[1] // 2
    size = share_out.shape[1]
    final = whole[...].astype(F32)
    for i in range(len(pieces) // 2):
        below, above = pieces[2 * i][...].astype(F32), pieces[2 * i + 1][...].astype(F32)
        none = jnp.zeros((final.shape[0], final.shape[1] - below.shape[1]), F32)
        final = final + jnp.concatenate([below, none], axis=1)
        final = final + jnp.concatenate([none, above], axis=1)
    tail[...] = final[:walkers, RADIUS * width : RADIUS * width + size].astype(BF16)
    row = info[0] - RADIUS + lax.broadcasted_iota(jnp.int32, (1, final.shape[1]), 1) // width
    ok = (row >= 0) & (row < info[1])
    total = jnp.where(ok, final[walkers : walkers + 1], 1.0)
    share = jnp.where(ok, final[:walkers] / total, 0.0).astype(BF16)
    window, step = band.shape[2], band.shape[1]
    value = collect(lambda p: share[:, p * step : p * step + window], band)
    back[...] = value
    total = begun[2 * walkers : 2 * walkers + 1]
    share = (value / total).astype(BF16)
    share_out[...] = share
    top[...] = share[:, : RADIUS * width]
    bottom[...] = share[:, size - RADIUS * width :]
    up, mid, down = adj_up[walkers:], adj_mid[walkers:], adj_down[walkers:]
    adjoint = joined(up, mid, down, width, walkers)
    loss = jnp.sum(share.astype(F32) * adjoint, axis=1, keepdims=True)
    carried[...] = jnp.where(info[2] == 1, scale[...], jnp.broadcast_to(loss, carried.shape))


def step_back_kernel(info, low, mid, high, band, begun, back, top, share_out, bottom):
    walkers = mid.shape[0]
    step, window = band.shape[1], band.shape[2]
    width = step // 2
    size = mid.shape[1]
    margin = jnp.concatenate([low[...], mid[...], high[...]], axis=1)
    value = collect(lambda p: margin[:, p * step : p * step + window], band)
    back[...] = value
    share = (value / begun[2 * walkers : 2 * walkers + 1]).astype(BF16)
    share_out[...] = share
    top[...] = share[:, : RADIUS * width]
    bottom[...] = share[:, size - RADIUS * width :]


def last_kernel(info, low, mid, high, band, first_band, begun, back, up, middle, down):
    walkers = mid.shape[0]
    step, window = band.shape[1], band.shape[2]
    margin = jnp.concatenate([low[...], mid[...], high[...]], axis=1)
    value = collect(lambda p: margin[:, p * step : p * step + window], band)
    back[...] = value
    share = (value / begun[2 * walkers : 2 * walkers + 1]).astype(BF16)
    split(spread(share, first_band), step // 2, up, middle, down)


def finish_kernel(groups, info, up, mid, down, tail, summed, *rest):
    backs, others = rest[: groups - 2], rest[groups - 2 : -2]
    returned, loss_out = rest[-2:]
    walkers, count, width = returned.shape
    time_index = info[2]
    own = summed[...]
    loss = jnp.where(time_index == groups - 2, own, 0.0)
    scale = jnp.where(time_index == 1, own, 0.0)
    for i, other in enumerate(others):
        source = lax.rem(time_index - i - 1 + groups, groups)
        loss = loss + jnp.where(source == groups - 2, other[...], 0.0)
        scale = scale + jnp.where(source == 1, other[...], 0.0)
    loss_out[...] = -jnp.log(loss / scale)
    value = jnp.where(
        time_index == 0, joined(up, mid, down, width, walkers), tail[...].astype(F32)
    )
    for i, back in enumerate(backs):
        value = jnp.where(time_index == i + 1, back[...], value)
    value = value / scale[:, :1]
    for a in range(count):
        returned[:, a, :] = value[:, a * width : (a + 1) * width]


def local(features, conv_weight, conv_bias, seed_nodes, targets):
    own = features[0]
    count, width, channels = own.shape
    groups = lax.axis_size("tm")
    bands = lax.axis_size("rows")
    time_index = lax.axis_index("tm")
    walkers = seed_nodes.shape[0]
    last = groups - 2
    edge, size = RADIUS * width, count * width
    info = jnp.stack(
        [lax.axis_index("rows") * count, jnp.int32(count * bands), time_index]
    ).astype(jnp.int32)

    same = [(t, t) for t in range(groups)]
    low = moved(own[count - LAYERS :], same, 1)
    high = moved(own[:LAYERS], same, -1)
    emb, emb_top, emb_bottom = encode(info, low, own, high, conv_weight, conv_bias)

    earlier = [(t - 1, t) for t in range(1, last + 1)]
    later = [(t + 1, t) for t in range(1, last + 1)]
    before = [moved(emb_bottom, earlier, 1), moved(emb, earlier, 0), moved(emb_top, earlier, -1)]
    after = [moved(emb_bottom, later, 1), moved(emb, later, 0), moved(emb_top, later, -1)]
    band_type = (band_shape(count, width), BF16)
    margin = pltpu.VMEM(((count + 2 * RADIUS) * width, channels), BF16)
    starts = jnp.concatenate([seed_nodes, targets, jnp.full((16,), -1, jnp.int32)])[:, None]
    first_band, begun = call(
        begin_kernel,
        [band_type, ((2 * walkers + 16, size), F32)],
        [emb, *before, starts],
        info,
        [margin],
        flops=2 * 10**9,
    )

    def cut(rows):
        return [((rows, edge), BF16), ((rows, size), BF16), ((rows, edge), BF16)]

    band, out_total, up, mid, down, scale = call(
        first_kernel,
        [band_type, ((8, size), F32), *cut(2 * walkers), ((walkers, width), F32)],
        [emb, *after, begun],
        info,
        [margin],
        flops=2 * 10**9,
    )
    parts = [moved(up, [(1, 2)], -1), moved(mid, [(1, 2)], 0), moved(down, [(1, 2)], 1)]

    span = (count + 2 * RADIUS) * width
    overlaps = []
    while span - size * (len(overlaps) + 1) > 0:
        overlaps.append(span - size * (len(overlaps) + 1))
    rows = walkers + 8
    whole, *pieces = call(
        turn_kernel,
        [((rows, span), BF16)] + [((rows, o), BF16) for o in overlaps for _ in range(2)],
        [*parts, band, out_total],
        info,
        flops=10**9,
    )
    here = [(last, last)]
    met = []
    for i in range(len(overlaps)):
        met.append(moved(pieces[2 * i], here, i + 1))
        met.append(moved(pieces[2 * i + 1], here, -i - 1))
    back, top, share, bottom, carried, tail = call(
        back_kernel,
        [((walkers, size), F32), *cut(walkers), ((walkers, width), F32), ((walkers, size), BF16)],
        [*parts, band, begun, scale, whole, *met],
        info,
        flops=10**9,
    )
    backs = [back]
    margins = [moved(bottom, [(2, 1)], 1), moved(share, [(2, 1)], 0), moved(top, [(2, 1)], -1)]
    tail = moved(tail, [(last, groups - 1)], 0)

    summed = carried
    for by in range(1, bands):
        pairs = [(r, (r + by) % bands) for r in range(bands)]
        summed = summed + lax.ppermute(carried, "rows", pairs)

    back, up, mid, down = call(
        last_kernel,
        [((walkers, size), F32), *cut(walkers)],
        [*margins, band, first_band, begun],
        info,
        flops=10**9,
    )
    backs.insert(0, back)
    parts = [moved(up, [(1, 0)], -1), moved(mid, [(1, 0)], 0), moved(down, [(1, 0)], 1)]
    others = []
    for by in range(1, groups):
        pairs = [(t, (t + by) % groups) for t in range(groups)]
        others.append(lax.ppermute(summed, "tm", pairs))
    returned, loss = call(
        functools.partial(finish_kernel, groups),
        [((walkers, count, width), F32), ((walkers, width), F32)],
        [*parts, tail, summed, *backs, *others],
        info,
        flops=10**6,
    )
    return (emb[None], returned[None], loss[:, 0])


def solution(mesh):
    placed = (P(("clips", "tm"), "rows", None, None), P(), P(), P("clips"), P("clips"))
    return jax.shard_map(
        local,
        mesh=mesh,
        in_specs=placed,
        out_specs=(
            P(("clips", "tm"), "rows", None, None),
            P("tm", "clips", "rows", None),
            P("clips"),
        ),
        check_vma=False,
    )
```
